256 devices in a mesh: dp: 16 (over x, z_lo), mp: 16 (over y, z_hi, core).
Axes of the slice: x: 4, y: 4, z: 8 (z_hi: 2, z_lo: 4; z = z_hi * 4 + z_lo), core: 2. Of those that a mesh axis runs over, the one named last changes fastest.
Arguments:
- tokens: bfloat16 [4096, 8192], P('dp', 'mp'), may hold values from -6 to 6
- cotangent: bfloat16 [4096, 14336], P('dp', 'mp'), may hold values from -6 to 6
- base_weight: bfloat16 [8192, 14336], P('dp', 'mp'), may hold values from -0.0625 to 0.0625
- shrink_weight: bfloat16 [4096, 8192], P(None, 'mp'), may hold values from -0.0625 to 0.0625
- expand_weight: bfloat16 [4096, 14336], P(None, 'mp'), may hold values from -0.09375 to 0.09375
- gates: float32 [8, 256], replicated, may hold values from -1 to 1
- segment_ids: int32 [4096], P('dp'), may hold values from 0 to 7, never falling along the last dimension, each value on 1 to 1024 neighbouring positions
Outputs:
- input_grad: float32 [4096, 8192], P('dp', 'mp')
- gate_grad: float32 [8, 256], P(None, 'mp')
The draws below stay inside these ranges and needn't reach their ends.
Inputs may be any that keep to these rules, and one draw needn't show every extreme that they name: `segment_ids`: segment numbers never fall along the tokens; each segment holds 1 to 1024 tokens and one holds exactly 1024.
All inputs are finite; a program needn't handle non-finite values.
Results may differ from the reference program's by a relative error of at most 0.0019.
Values may be sent and summed in bfloat16 or wider, within the bound.
No kernel may reach another device: no remote copies, remote signals or barrier semaphores. Data moves between devices by JAX's collectives and lax.ppermute only.
A program may use at most 128 MiB of HBM per device.

```python
import math
import jax
import jax.numpy as jnp
import numpy as np
from jax import lax

D = 8192
F = 14336
NA = 256
RANK = 16
NSEG = 8
TOKENS = 4096
R = 4096
SEG_MOST = 1024


def steps_of(key, shape, pieces, smallest, top_value):
    factor_of, own = 1.0, jax.random.fold_in(key, 6)
    for position, parts in pieces:
        steps = jnp.exp(jax.random.uniform(jax.random.fold_in(own, position), (parts,), jnp.float32, smallest / len(pieces), top_value / len(pieces)))
        factor_of = factor_of * jnp.repeat(steps, shape[position] // parts).reshape([-1 if axis == position else 1 for axis in range(len(shape))])
    return factor_of


def profile(amount, total, most, skew):
    loads = [(1 << 20) // math.isqrt(standing ** skew) + 1 for standing in range(2, amount + 1)]
    spare, holding = total - most - (amount - 1), [1] * (amount - 1)
    while spare > 0:
        candidates = [i for i in range(amount - 1) if holding[i] < most]
        whole, budget = sum([loads[i] for i in candidates]), spare
        for i in candidates:
            more = min(most - holding[i], max(1, budget * loads[i] // whole), spare)
            holding[i] = holding[i] + more
            spare = spare - more
    return np.array([most] + holding)


def uneven_parts(stream_key, count, total, bound, lean):
    if count == 2:
        one = jax.random.randint(stream_key, (), max(1, total - bound), min(bound, total - 1) + 1)
        return jnp.stack([one, total - one])
    tallies = jnp.asarray(profile(count, total, bound, lean), jnp.int32)
    pairs = (count - 1) // 2
    source_of, receiver = tallies[1:1 + 2 * pairs:2], tallies[2:2 + 2 * pairs:2]
    margin = jnp.minimum(source_of - 1, bound - receiver)
    passed = jax.random.randint(jax.random.fold_in(stream_key, 1), (pairs,), 0, 1 << 20) % (margin + 1)
    tallies = tallies.at[1:1 + 2 * pairs:2].set(source_of - passed).at[2:2 + 2 * pairs:2].set(receiver + passed)
    return tallies[jax.random.permutation(jax.random.fold_in(stream_key, 2), count)]


def centred(rng, shape, width, limit, shards=(), held_as=jnp.bfloat16):
    loudness = steps_of(rng, shape, shards, -0.22, 0.18) if shards else 1.0
    drawn = jax.random.normal(rng, shape, jnp.float32) * width * loudness
    return jnp.minimum(jnp.maximum(drawn, -limit), limit).astype(held_as)


def setup_inputs(seed: int = 0) -> dict:
    splits = jax.random.split(jax.random.key(seed), 8)
    return {
        "tokens": centred(splits[0], (TOKENS, D), 1.0, 6.0, ((0, 16), (1, 16))),
        "cotangent": centred(splits[1], (TOKENS, F), 1.0, 6.0, ((0, 16), (1, 16))),
        "base_weight": centred(splits[2], (D, F), D ** -0.5, 0.0625, ((0, 16), (1, 16))),
        "shrink_weight": centred(splits[3], (R, D), D ** -0.5, 0.0625, ((1, 16),)),
        "expand_weight": centred(splits[4], (R, F), R ** -0.5, 0.09375, ((1, 16),)),
        "gates": jnp.clip(jax.random.uniform(splits[5], (NSEG, NA), jnp.float32, -1.0, 1.0), -1.0, 1.0),
        "segment_ids": jnp.searchsorted(jnp.cumsum(uneven_parts(splits[6], NSEG, TOKENS, SEG_MOST, 2)), jnp.arange(TOKENS), side="right").astype(jnp.int32),
    }


def reference(tokens, cotangent, base_weight, shrink_weight, expand_weight, gates, segment_ids):
    count = tokens.shape[0]
    onehot = (segment_ids[:, None] == jnp.arange(NSEG, dtype=jnp.int32)[None, :]).astype(jnp.float32)
    token_gate = jnp.dot(onehot, gates, precision=lax.Precision.HIGHEST)
    shrunk = jnp.dot(tokens, shrink_weight.T, preferred_element_type=jnp.float32)
    pulled = jnp.dot(cotangent, expand_weight.T, preferred_element_type=jnp.float32)
    scaled = (pulled.reshape(count, NA, RANK) * token_gate[:, :, None]).reshape(count, R).astype(jnp.bfloat16)
    base = jnp.dot(cotangent, base_weight.T, preferred_element_type=jnp.float32)
    low_rank = jnp.dot(scaled, shrink_weight, preferred_element_type=jnp.float32)
    input_grad = base + low_rank
    per_token = (shrunk * pulled).reshape(count, NA, RANK).sum(axis=2)
    gate_grad = jnp.dot(onehot.T, per_token, precision=lax.Precision.HIGHEST)
    return input_grad, gate_grad
```

```python
import jax
import jax.numpy as jnp
from jax import lax
from jax.sharding import Mesh, PartitionSpec as P

RANK = 16
AXES = ("x", "l", "y", "h", "c")
SIZES = (4, 4, 4, 2, 2)
HALF = jnp.float16
SCALE = 8.0


def contract_last(left, right):
    return lax.dot_general(
        left, right, (((1,), (1,)), ((), ())), preferred_element_type=jnp.float32
    )


def shift(value, axis, by):
    return lax.ppermute(value, axis, [(i, (i + by) % 4) for i in range(4)])


def swap(value, axis):
    return lax.ppermute(value, axis, [(0, 1), (1, 0)])


def rows(value, block, count):
    return lax.dynamic_slice_in_dim(value, block * count, count, 0)


def packed(value):
    return (value * SCALE).astype(HALF)


def unpacked(value):
    return value.astype(jnp.float32) * (1.0 / SCALE)


def gather_pulled(cotangent, expand_weight, y, c):
    partial = contract_last(expand_weight, cotangent)
    half = partial.shape[0] // 2
    mine = rows(partial, c, half) + swap(rows(partial, 1 - c, half), "c")
    quarter = half // 4
    parts = [shift(packed(rows(mine, (y + s) % 4, quarter)), "y", s) for s in (2, 1, 3)]
    mine = rows(mine, y, quarter) + (unpacked(parts[0]) + unpacked(parts[1]) + unpacked(parts[2]))
    mine = mine + unpacked(swap(packed(mine), "h"))
    own = packed(mine)
    back = [own] + [shift(own, "y", s) for s in (1, 2, 3)]
    order = jnp.concatenate([back[(3 - p) % 4] for p in range(7)], axis=0)
    mine = lax.dynamic_slice_in_dim(order, (3 - y) * quarter, half, 0)
    other = swap(mine, "c")
    return unpacked(
        jnp.concatenate([jnp.where(c == 0, mine, other), jnp.where(c == 0, other, mine)], axis=0)
    )


def reduce_gates(partial, y, h, c):
    quarter = partial.shape[0] // 4
    got = [shift(rows(partial, (y + s) % 4, quarter), "y", s) for s in (1, 2, 3)]
    partial = (rows(partial, y, quarter) + got[1]) + (got[0] + got[2])
    place = 2 * h + c
    share = quarter // 4
    got = [shift(rows(partial, (place + s) % 4, share), ("h", "c"), s) for s in (1, 2, 3)]
    partial = (rows(partial, place, share) + got[1]) + (got[0] + got[2])
    for axis in ("x", "l"):
        got = [shift(partial, axis, s) for s in (1, 2, 3)]
        partial = (partial + got[1]) + (got[0] + got[2])
    return partial


def gather_weight(base_weight, c):
    half = base_weight.shape[0] // 2
    own = rows(base_weight, c, half)
    other = swap(rows(base_weight, 1 - c, half), "c")
    own_before, own_after = shift(own, "x", 1), shift(own, "x", -1)
    other_before, other_after = shift(other, "x", 1), shift(other, "x", -1)
    own_far = shift(own_before, "x", 1)
    other_far = shift(other_after, "x", -1)
    return [(own, other), (own_before, other_before), (own_far, other_far), (own_after, other_after)]


def base_gradient(cotangent, base_weight, x, l, y, h, c):
    width = cotangent.shape[0]
    own = [cotangent] + [shift(cotangent, "l", s) for s in (1, 2, 3)]
    other = [swap(block, "c") for block in own]
    own, other = jnp.concatenate(own, axis=0), jnp.concatenate(other, axis=0)
    blocks = [
        packed(contract_last(own, w_own) + contract_last(other, w_other))
        for w_own, w_other in gather_weight(base_weight, c)
    ]
    blocks = jnp.concatenate(blocks, axis=0)
    tall = own.shape[0]
    got = [shift(rows(blocks, (x - y - s) % 4, tall), "y", s) for s in (2, 1, 3)]
    total = rows(blocks, (x - y) % 4, tall).astype(jnp.float32)
    total = total + (got[0].astype(jnp.float32) + got[1].astype(jnp.float32) + got[2].astype(jnp.float32))
    total = total.astype(HALF)
    place = 2 * h + c
    got = []
    for k in range(4):
        target = (place + k) % 4
        perm = [
            (ll * 4 + p, ((p + k) % 4) * 4 + ll) for ll in range(4) for p in range(4)
        ]
        got.append(unpacked(lax.ppermute(rows(total, (l - target) % 4, width), ("l", "h", "c"), perm)))
    even, odd = got[0] + got[2], got[1] + got[3]
    flip = l % 2 == 1
    return jnp.concatenate([jnp.where(flip, odd, even), jnp.where(flip, even, odd)], axis=1)


def on_device(tokens, cotangent, base_weight, shrink_weight, expand_weight, gates, segment_ids):
    x, l, y, h, c = (lax.axis_index(a) for a in AXES)
    onehot = (segment_ids[:, None] == jnp.arange(gates.shape[0], dtype=jnp.int32)[None, :]).astype(
        jnp.float32
    )
    base = base_gradient(cotangent, base_weight, x, l, y, h, c)
    pulled = gather_pulled(cotangent, expand_weight, y, c)
    gate_rows = jnp.repeat(gates.T, RANK, axis=0)
    token_gate = jnp.dot(gate_rows, onehot.T, precision=lax.Precision.HIGHEST)
    scaled = (pulled * token_gate).astype(jnp.bfloat16)
    shrunk = contract_last(shrink_weight, tokens)
    per_token = (shrunk * pulled).reshape(-1, RANK, tokens.shape[0]).sum(axis=1)
    gate_grad = reduce_gates(
        jnp.dot(per_token, onehot, precision=lax.Precision.HIGHEST), y, h, c
    )
    low_rank = lax.dot_general(
        scaled, shrink_weight, (((0,), (0,)), ((), ())), preferred_element_type=jnp.float32
    )
    return (base + low_rank, gate_grad.T)


def solution(mesh):
    fine = Mesh(mesh.devices.reshape(SIZES), AXES)
    dp, mp = ("x", "l"), ("y", "h", "c")
    in_specs = (P(dp, mp), P(dp, mp), P(dp, mp), P(None, mp), P(None, mp), P(), P(dp))
    out_specs = (P(dp, mp), P(None, mp))
    return jax.shard_map(
        on_device, mesh=fine, in_specs=in_specs, out_specs=out_specs, check_vma=False
    )
```

```python
import jax
import jax.numpy as jnp
from jax import lax
from jax.sharding import Mesh, PartitionSpec as P

RANK = 16
AXES = ("x", "l", "y", "h", "c")
SIZES = (4, 4, 4, 2, 2)
HALF = jnp.float16
SCALE = 8.0
GATED = 4


def contract_last(left, right):
    return lax.dot_general(
        left, right, (((1,), (1,)), ((), ())), preferred_element_type=jnp.float32
    )


def shift(value, axis, by):
    return lax.ppermute(value, axis, [(i, (i + by) % 4) for i in range(4)])


def partner(value, axis):
    return lax.ppermute(value, axis, [(0, 1), (1, 0)])


def packed(value):
    return (value * SCALE).astype(HALF)


def wide(value):
    return value.astype(jnp.float32)


def rows(value, block, count):
    return lax.dynamic_slice_in_dim(value, block * count, count, 0)


def barrier(*values):
    return lax.optimization_barrier(values)


def everyone(value, axis):
    got = [shift(value, axis, s) for s in (1, 2, 3)]
    return (value + got[1]) + (got[0] + got[2])


def on_device(tokens, cotangent, base_weight, shrink_weight, expand_weight, gates, segment_ids):
    x, l, y, h, c = (lax.axis_index(a) for a in AXES)
    width, columns = cotangent.shape
    half = base_weight.shape[0] // 2
    ranks = expand_weight.shape[0]
    share = ranks // 16
    tall = 4 * width

    whole = lax.all_to_all(jnp.broadcast_to(cotangent[None], (4, width, columns)), "l", 0, 0)
    w_before, w_after = barrier(shift(base_weight, "x", 1), shift(base_weight, "x", -1))

    def over_core(partial):
        count = ranks // 2
        got = partner(rows(partial, 1 - c, count), "c")
        return (wide(rows(partial, c, count)) + wide(got)).astype(HALF)

    def over_y(mine):
        return [shift(rows(mine, (y + s) % 4, 2 * share), "y", s) for s in (2, 1, 3)]

    def summed(own, got):
        return ((wide(own) + wide(got[0])) + (wide(got[1]) + wide(got[2]))).astype(HALF)

    pulled = over_core(packed(contract_last(expand_weight, cotangent)))

    far_keep = shift(rows(w_before, c, half), "x", 1)
    far_away = shift(rows(w_after, 1 - c, half), "x", -1)

    pulled = summed(rows(pulled, y, 2 * share), over_y(pulled))
    shrunk = over_core(packed(contract_last(shrink_weight, tokens)))
    whole, pulled, shrunk, far_keep, far_away = barrier(whole, pulled, shrunk, far_keep, far_away)
    whole = whole.reshape(tall, columns)
    got = partner(pulled, "h")
    s_got = over_y(shrunk)

    def weights(side, far_block):
        near = [rows(v, side, half) for v in (base_weight, w_before, w_after)]
        return barrier(jnp.concatenate([*near, far_block], axis=0))[0]

    away = partner(packed(contract_last(whole, weights(1 - c, far_away))), "c")
    kept = (contract_last(whole, weights(c, far_keep)) * SCALE + wide(away)).astype(HALF)
    kept, got, *s_got = barrier(kept, got, *s_got)
    pulled = pulled + got

    def column(s):
        r = (x - y - s) % 4
        return lax.dynamic_slice_in_dim(kept, jnp.where(r < 2, r, 5 - r) * half, half, 1)

    sent = [
        shift(jnp.concatenate([column(s), pulled], axis=0), "y", s) for s in (2, 1, 3)
    ]
    onehot = (segment_ids[:, None] == jnp.arange(gates.shape[0], dtype=jnp.int32)[None, :]).astype(
        jnp.float32
    )
    shrunk = summed(rows(shrunk, y, 2 * share), s_got)
    grad = wide(shrunk) * wide(pulled) * (1.0 / SCALE**2)
    grad = jnp.dot(grad, onehot, precision=lax.Precision.HIGHEST)
    grad = grad.reshape(-1, RANK, gates.shape[0]).sum(axis=1)
    grad = everyone(everyone(grad, "x"), "l")
    own, other = [
        lax.ppermute(
            rows(grad, jnp.where(flip == 0, h, 1 - h), share // RANK),
            ("y", "h", "c"),
            [(i, i % 2 * 8 + i // 4 * 2 + (i // 2 % 2 ^ flip)) for i in range(16)],
        )
        for flip in (0, 1)
    ]
    grad = own + other

    *sent, grad = barrier(*sent, grad)
    total = wide(column(0)) + wide(sent[0][:tall])
    total = (total + (wide(sent[1][:tall]) + wide(sent[2][:tall]))).astype(HALF)
    total, *sent = barrier(total, *sent)
    blocks = [v[tall:] for v in sent]
    place = 2 * h + c
    moved = []
    for k in range(4):
        perm = [(ll * 4 + p, ((p + k) % 4) * 4 + ll) for ll in range(4) for p in range(4)]
        moved.append(lax.ppermute(rows(total, (place + k) % 4, width), ("l", "h", "c"), perm))

    mine = jnp.concatenate([pulled, blocks[1], blocks[0], blocks[2]], axis=0)
    got = partner(mine, "c")
    got, *moved[:GATED] = barrier(got, *moved[:GATED])
    def low_rank(core, pulled):
        def turned(value, count):
            return jnp.concatenate([rows(value, core * 4 + (y - s) % 4, count) for s in range(4)])

        gate_rows = jnp.repeat(turned(gates.T, 2 * share // RANK), RANK, axis=0)
        token_gate = jnp.dot(gate_rows, onehot.T, precision=lax.Precision.HIGHEST)
        scaled = (wide(pulled) * (1.0 / SCALE) * token_gate).astype(jnp.bfloat16)
        return lax.dot_general(
            scaled,
            turned(shrink_weight, 2 * share),
            (((0,), (0,)), ((), ())),
            preferred_element_type=jnp.float32,
        )

    low_rank = low_rank(c, mine) + low_rank(1 - c, got)
    moved = [wide(v) * (1.0 / SCALE) for v in moved]
    even, odd = moved[0] + moved[2], moved[1] + moved[3]
    flip = l % 2 == 1
    base = jnp.concatenate([jnp.where(flip, odd, even), jnp.where(flip, even, odd)], axis=1)
    return (base + low_rank, grad.T)


def solution(mesh):
    fine = Mesh(mesh.devices.reshape(SIZES), AXES)
    dp, mp = ("x", "l"), ("y", "h", "c")
    in_specs = (P(dp, mp), P(dp, mp), P(dp, mp), P(None, mp), P(None, mp), P(), P(dp))
    out_specs = (P(dp, mp), P(None, mp))
    return jax.shard_map(
        on_device, mesh=fine, in_specs=in_specs, out_specs=out_specs, check_vma=False
    )
```

```python
import jax
import jax.numpy as jnp
from jax import lax
from jax.sharding import Mesh, PartitionSpec as P

RANK = 16
AXES = ("x", "l", "y", "h", "c")
SIZES = (4, 4, 4, 2, 2)
HALF = jnp.float16
SCALE = 8.0


def contract_last(left, right):
    return lax.dot_general(
        left, right, (((1,), (1,)), ((), ())), preferred_element_type=jnp.float32
    )


def shift(value, axis, by):
    return lax.ppermute(value, axis, [(i, (i + by) % 4) for i in range(4)])


def partner(value, axis):
    return lax.ppermute(value, axis, [(0, 1), (1, 0)])


def packed(value):
    return (value * SCALE).astype(HALF)


def wide(value):
    return value.astype(jnp.float32)


def rows(value, block, count):
    return lax.dynamic_slice_in_dim(value, block * count, count, 0)


def barrier(*values):
    return lax.optimization_barrier(values)


def everyone(value, axis):
    got = [shift(value, axis, s) for s in (1, 2, 3)]
    return (value + got[1]) + (got[0] + got[2])


def on_device(tokens, cotangent, base_weight, shrink_weight, expand_weight, gates, segment_ids):
    x, l, y, h, c = (lax.axis_index(a) for a in AXES)
    width, columns = cotangent.shape
    half = base_weight.shape[0] // 2
    ranks = expand_weight.shape[0]
    share = ranks // 16
    tall = 4 * width

    whole = lax.all_to_all(jnp.broadcast_to(cotangent[None], (4, width, columns)), "l", 0, 0)
    w_before, w_after = barrier(shift(base_weight, "x", 1), shift(base_weight, "x", -1))

    def over_core(partial):
        count = ranks // 2
        got = partner(rows(partial, 1 - c, count), "c")
        return (wide(rows(partial, c, count)) + wide(got)).astype(HALF)

    def over_y(mine):
        return [shift(rows(mine, (y + s) % 4, 2 * share), "y", s) for s in (2, 1, 3)]

    def summed(own, got):
        return ((wide(own) + wide(got[0])) + (wide(got[1]) + wide(got[2]))).astype(HALF)

    pulled = over_core(packed(contract_last(expand_weight, cotangent)))

    far_keep = shift(rows(w_before, c, half), "x", 1)
    far_away = shift(rows(w_after, 1 - c, half), "x", -1)

    pulled = summed(rows(pulled, y, 2 * share), over_y(pulled))
    shrunk = over_core(packed(contract_last(shrink_weight, tokens)))
    def weights(side, far_block):
        near = [rows(v, side, half) for v in (base_weight, w_before, w_after)]
        return barrier(jnp.concatenate([*near, far_block], axis=0))[0]

    whole, pulled, shrunk, far_keep, far_away = barrier(whole, pulled, shrunk, far_keep, far_away)
    keep_own, keep_other = weights(c, far_keep), partner(weights(1 - c, far_away), "c")
    whole = whole.reshape(tall, columns)
    got = partner(pulled, "h")
    s_got = over_y(shrunk)

    kept = contract_last(whole, keep_own) + contract_last(partner(whole, "c"), keep_other)
    kept = packed(kept)
    kept, got, *s_got = barrier(kept, got, *s_got)
    pulled = pulled + got

    def column(s):
        r = (x - y - s) % 4
        return lax.dynamic_slice_in_dim(kept, jnp.where(r < 2, r, 5 - r) * half, half, 1)

    sent = [
        shift(jnp.concatenate([column(s), pulled], axis=0), "y", s) for s in (2, 1, 3)
    ]
    onehot = (segment_ids[:, None] == jnp.arange(gates.shape[0], dtype=jnp.int32)[None, :]).astype(
        jnp.float32
    )
    shrunk = summed(rows(shrunk, y, 2 * share), s_got)
    grad = wide(shrunk) * wide(pulled) * (1.0 / SCALE**2)
    grad = jnp.dot(grad, onehot, precision=lax.Precision.HIGHEST)
    grad = grad.reshape(-1, RANK, gates.shape[0]).sum(axis=1)
    grad = everyone(everyone(grad, "x"), "l")
    own, other = [
        lax.ppermute(
            rows(grad, jnp.where(flip == 0, h, 1 - h), share // RANK),
            ("y", "h", "c"),
            [(i, i % 2 * 8 + i // 4 * 2 + (i // 2 % 2 ^ flip)) for i in range(16)],
        )
        for flip in (0, 1)
    ]
    grad = own + other

    *sent, grad = barrier(*sent, grad)
    own = column(0)
    place = 2 * h + c
    moved = []
    for k in range(4):
        perm = [(ll * 4 + p, ((p + k) % 4) * 4 + ll) for ll in range(4) for p in range(4)]
        own_rows, *got_rows = [rows(v, (place + k) % 4, width) for v in (own, *sent)]
        moved.append(lax.ppermute(summed(own_rows, got_rows), ("l", "h", "c"), perm))
    moved[0], *sent = barrier(moved[0], *sent)
    blocks = [v[tall:] for v in sent]
    mine = jnp.concatenate([pulled, blocks[1], blocks[0], blocks[2]], axis=0)
    got = partner(mine, "c")
    def low_rank(core, pulled):
        def turned(value, count):
            return jnp.concatenate([rows(value, core * 4 + (y - s) % 4, count) for s in range(4)])

        gate_rows = jnp.repeat(turned(gates.T, 2 * share // RANK), RANK, axis=0)
        token_gate = jnp.dot(gate_rows, onehot.T, precision=lax.Precision.HIGHEST)
        scaled = (wide(pulled) * (1.0 / SCALE) * token_gate).astype(jnp.bfloat16)
        return lax.dot_general(
            scaled,
            turned(shrink_weight, 2 * share),
            (((0,), (0,)), ((), ())),
            preferred_element_type=jnp.float32,
        )

    low_rank = low_rank(c, mine) + low_rank(1 - c, got)
    moved = [wide(v) * (1.0 / SCALE) for v in moved]
    even, odd = moved[0] + moved[2], moved[1] + moved[3]
    flip = l % 2 == 1
    base = jnp.concatenate([jnp.where(flip, odd, even), jnp.where(flip, even, odd)], axis=1)
    return (base + low_rank, grad.T)


def solution(mesh):
    fine = Mesh(mesh.devices.reshape(SIZES), AXES)
    dp, mp = ("x", "l"), ("y", "h", "c")
    in_specs = (P(dp, mp), P(dp, mp), P(dp, mp), P(None, mp), P(None, mp), P(), P(dp))
    out_specs = (P(dp, mp), P(None, mp))
    return jax.shard_map(
        on_device, mesh=fine, in_specs=in_specs, out_specs=out_specs, check_vma=False
    )
```

```python
import jax
import jax.numpy as jnp
from jax import lax
from jax.sharding import Mesh, PartitionSpec as P

RANK = 16
AXES = ("x", "l", "y", "h", "c")
SIZES = (4, 4, 4, 2, 2)
HALF = jnp.float16
PULLED, SHRUNK, BASE = 128.0, 256.0, 64.0


def contract_last(left, right):
    return lax.dot_general(
        left, right, (((1,), (1,)), ((), ())), preferred_element_type=jnp.float32
    )


def shift(value, axis, by):
    return lax.ppermute(value, axis, [(i, (i + by) % 4) for i in range(4)])


def partner(value, axis):
    return lax.ppermute(value, axis, [(0, 1), (1, 0)])


def packed(value, scale):
    return (value * scale).astype(HALF)


def wide(value):
    return value.astype(jnp.float32)


def rows(value, block, count):
    return lax.dynamic_slice_in_dim(value, block * count, count, 0)


def barrier(*values):
    return lax.optimization_barrier(values)


def everyone(value, axis):
    got = [shift(value, axis, s) for s in (1, 2, 3)]
    return (value + got[1]) + (got[0] + got[2])


def on_device(tokens, cotangent, base_weight, shrink_weight, expand_weight, gates, segment_ids):
    x, l, y, h, c = (lax.axis_index(a) for a in AXES)
    width, columns = cotangent.shape
    half = base_weight.shape[0] // 2
    ranks = expand_weight.shape[0]
    share = ranks // 16
    tall = 4 * width

    whole = lax.all_to_all(jnp.broadcast_to(cotangent[None], (4, width, columns)), "l", 0, 0)
    w_before, w_after = barrier(shift(base_weight, "x", 1), shift(base_weight, "x", -1))

    def over_core(partial):
        count = ranks // 2
        got = partner(rows(partial, 1 - c, count), "c")
        return packed(wide(rows(partial, c, count)) + wide(got), 0.5)

    def over_y(mine):
        return [shift(rows(mine, (y + s) % 4, 2 * share), "y", s) for s in (2, 1, 3)]

    def summed(own, got):
        return packed((wide(own) + wide(got[0])) + (wide(got[1]) + wide(got[2])), 0.25)

    pulled = over_core(packed(contract_last(expand_weight, cotangent), PULLED))

    far_keep = shift(rows(w_before, c, half), "x", 1)
    far_away = shift(rows(w_after, 1 - c, half), "x", -1)

    pulled = summed(rows(pulled, y, 2 * share), over_y(pulled))
    shrunk = over_core(packed(contract_last(shrink_weight, tokens), SHRUNK))
    def weights(side, far_block):
        near = [rows(v, side, half) for v in (base_weight, w_before, w_after)]
        return barrier(jnp.concatenate([*near, far_block], axis=0))[0]

    whole, pulled, shrunk, far_keep, far_away = barrier(whole, pulled, shrunk, far_keep, far_away)
    keep_own, keep_other = weights(c, far_keep), partner(weights(1 - c, far_away), "c")
    whole = whole.reshape(tall, columns)
    got = partner(pulled, "h")
    s_got = over_y(shrunk)

    kept = contract_last(whole, keep_own) + contract_last(partner(whole, "c"), keep_other)
    kept = packed(kept, BASE)
    kept, got, *s_got = barrier(kept, got, *s_got)
    pulled = packed(wide(pulled) + wide(got), 0.5)

    def column(s):
        r = (x - y - s) % 4
        return lax.dynamic_slice_in_dim(kept, jnp.where(r < 2, r, 5 - r) * half, half, 1)

    sent = [
        shift(jnp.concatenate([column(s), pulled], axis=0), "y", s) for s in (2, 1, 3)
    ]
    onehot = (segment_ids[:, None] == jnp.arange(gates.shape[0], dtype=jnp.int32)[None, :]).astype(
        jnp.float32
    )
    shrunk = summed(rows(shrunk, y, 2 * share), s_got)
    grad = wide(shrunk) * wide(pulled) * (128.0 / (PULLED * SHRUNK))
    grad = jnp.dot(grad, onehot, precision=lax.Precision.HIGHEST)
    grad = grad.reshape(-1, RANK, gates.shape[0]).sum(axis=1)
    grad = everyone(everyone(grad, "x"), "l")
    own, other = [
        lax.ppermute(
            rows(grad, jnp.where(flip == 0, h, 1 - h), share // RANK),
            ("y", "h", "c"),
            [(i, i % 2 * 8 + i // 4 * 2 + (i // 2 % 2 ^ flip)) for i in range(16)],
        )
        for flip in (0, 1)
    ]
    grad = own + other

    *sent, grad = barrier(*sent, grad)
    own = column(0)
    place = 2 * h + c
    moved = []
    for k in range(4):
        perm = [(ll * 4 + p, ((p + k) % 4) * 4 + ll) for ll in range(4) for p in range(4)]
        own_rows, *got_rows = [rows(v, (place + k) % 4, width) for v in (own, *sent)]
        moved.append(lax.ppermute(summed(own_rows, got_rows), ("l", "h", "c"), perm))
    moved[0], *sent = barrier(moved[0], *sent)
    blocks = [v[tall:] for v in sent]
    mine = jnp.concatenate([pulled, blocks[1], blocks[0], blocks[2]], axis=0)
    got = partner(mine, "c")
    def low_rank(core, pulled):
        def turned(value, count):
            return jnp.concatenate([rows(value, core * 4 + (y - s) % 4, count) for s in range(4)])

        gate_rows = jnp.repeat(turned(gates.T, 2 * share // RANK), RANK, axis=0)
        token_gate = jnp.dot(gate_rows, onehot.T, precision=lax.Precision.HIGHEST)
        scaled = (wide(pulled) * (16.0 / PULLED) * token_gate).astype(jnp.bfloat16)
        return lax.dot_general(
            scaled,
            turned(shrink_weight, 2 * share),
            (((0,), (0,)), ((), ())),
            preferred_element_type=jnp.float32,
        )

    low_rank = low_rank(c, mine) + low_rank(1 - c, got)
    moved = [wide(v) * (4.0 / BASE) for v in moved]
    even, odd = moved[0] + moved[2], moved[1] + moved[3]
    flip = l % 2 == 1
    base = jnp.concatenate([jnp.where(flip, odd, even), jnp.where(flip, even, odd)], axis=1)
    return (base + low_rank, grad.T)


def solution(mesh):
    fine = Mesh(mesh.devices.reshape(SIZES), AXES)
    dp, mp = ("x", "l"), ("y", "h", "c")
    in_specs = (P(dp, mp), P(dp, mp), P(dp, mp), P(None, mp), P(None, mp), P(), P(dp))
    out_specs = (P(dp, mp), P(None, mp))
    return jax.shard_map(
        on_device, mesh=fine, in_specs=in_specs, out_specs=out_specs, check_vma=False
    )
```

```python
import jax
import jax.numpy as jnp
from jax import lax
from jax.sharding import Mesh, PartitionSpec as P

RANK = 16
AXES = ("x", "l", "y", "h", "c")
SIZES = (4, 4, 4, 2, 2)
HALF = jnp.float16
PULLED, SHRUNK, BASE = 128.0, 256.0, 64.0


def contract_last(left, right):
    return lax.dot_general(
        left, right, (((1,), (1,)), ((), ())), preferred_element_type=jnp.float32
    )


def shift(value, axis, by):
    return lax.ppermute(value, axis, [(i, (i + by) % 4) for i in range(4)])


def partner(value, axis):
    return lax.ppermute(value, axis, [(0, 1), (1, 0)])


def packed(value, scale):
    return (value * scale).astype(HALF)


def wide(value):
    return value.astype(jnp.float32)


def rows(value, block, count):
    return lax.dynamic_slice_in_dim(value, block * count, count, 0)


def barrier(*values):
    return lax.optimization_barrier(values)


def everyone(value, axis):
    for flip in (1, 2):
        value = value + lax.ppermute(value, axis, [(i, i ^ flip) for i in range(4)])
    return value


def on_device(tokens, cotangent, base_weight, shrink_weight, expand_weight, gates, segment_ids):
    x, l, y, h, c = (lax.axis_index(a) for a in AXES)
    width, columns = cotangent.shape
    half = base_weight.shape[0] // 2
    ranks = expand_weight.shape[0]
    share = ranks // 16
    tall = 4 * width

    whole = lax.all_to_all(jnp.broadcast_to(cotangent[None], (4, width, columns)), "l", 0, 0)
    w_before, w_after = barrier(shift(base_weight, "x", 1), shift(base_weight, "x", -1))

    def over_core(partial):
        count = ranks // 2
        got = partner(rows(partial, 1 - c, count), "c")
        return packed(wide(rows(partial, c, count)) + wide(got), 0.5)

    def over_y(mine):
        return [shift(rows(mine, (y + s) % 4, 2 * share), "y", s) for s in (2, 1, 3)]

    def summed(own, got):
        return packed((wide(own) + wide(got[0])) + (wide(got[1]) + wide(got[2])), 0.25)

    pulled = over_core(packed(contract_last(expand_weight, cotangent), PULLED))

    far_keep = shift(rows(w_before, c, half), "x", 1)
    far_away = shift(rows(w_after, 1 - c, half), "x", -1)

    pulled = summed(rows(pulled, y, 2 * share), over_y(pulled))
    shrunk = over_core(packed(contract_last(shrink_weight, tokens), SHRUNK))
    def weights(side, far_block):
        near = [rows(v, side, half) for v in (base_weight, w_before, w_after)]
        return barrier(jnp.concatenate([*near, far_block], axis=0))[0]

    whole, pulled, shrunk, far_keep, far_away = barrier(whole, pulled, shrunk, far_keep, far_away)
    keep_own, keep_other = weights(c, far_keep), partner(weights(1 - c, far_away), "c")
    whole = whole.reshape(tall, columns)
    got = partner(pulled, "h")
    s_got = over_y(shrunk)

    kept = contract_last(whole, keep_own) + contract_last(partner(whole, "c"), keep_other)
    kept = packed(kept, BASE)
    kept, got, *s_got = barrier(kept, got, *s_got)
    pulled = packed(wide(pulled) + wide(got), 0.5)

    def column(s):
        r = (x - y - s) % 4
        return lax.dynamic_slice_in_dim(kept, jnp.where(r < 2, r, 5 - r) * half, half, 1)

    sent = [
        shift(jnp.concatenate([pulled, column(s)], axis=0), "y", s) for s in (2, 1, 3)
    ]
    onehot = (segment_ids[:, None] == jnp.arange(gates.shape[0], dtype=jnp.int32)[None, :]).astype(
        jnp.float32
    )
    shrunk = summed(rows(shrunk, y, 2 * share), s_got)
    grad = wide(shrunk) * wide(pulled) * (128.0 / (PULLED * SHRUNK))
    grad = jnp.dot(grad, onehot, precision=lax.Precision.HIGHEST)
    grad = grad.reshape(-1, RANK, gates.shape[0]).sum(axis=1)
    grad = everyone(everyone(grad, "x"), "l")
    own, other = [
        lax.ppermute(
            rows(grad, jnp.where(flip == 0, h, 1 - h), share // RANK),
            ("y", "h", "c"),
            [(i, i % 2 * 8 + i // 4 * 2 + (i // 2 % 2 ^ flip)) for i in range(16)],
        )
        for flip in (0, 1)
    ]
    grad = own + other

    *sent, grad = barrier(*sent, grad)
    own = column(0)
    place = 2 * h + c
    moved = []
    for k in range(4):
        perm = [(ll * 4 + p, ((p + k) % 4) * 4 + ll) for ll in range(4) for p in range(4)]
        own_rows, *got_rows = [rows(own, (place + k) % 4, width)] + [
            rows(v, (place + k) % 4 + 2, width) for v in sent
        ]
        moved.append(lax.ppermute(summed(own_rows, got_rows), ("l", "h", "c"), perm))
    moved[0], *sent = barrier(moved[0], *sent)
    blocks = [v[: 2 * share] for v in sent]
    mine = jnp.concatenate([pulled, blocks[1], blocks[0], blocks[2]], axis=0)
    got = partner(mine, "c")
    def low_rank(core, pulled):
        def turned(value, count):
            return jnp.concatenate([rows(value, core * 4 + (y - s) % 4, count) for s in range(4)])

        gate_rows = jnp.repeat(turned(gates.T, 2 * share // RANK), RANK, axis=0)
        token_gate = jnp.dot(gate_rows, onehot.T, precision=lax.Precision.HIGHEST)
        scaled = (wide(pulled) * (16.0 / PULLED) * token_gate).astype(jnp.bfloat16)
        return lax.dot_general(
            scaled,
            turned(shrink_weight, 2 * share),
            (((0,), (0,)), ((), ())),
            preferred_element_type=jnp.float32,
        )

    half_done, got = barrier(low_rank(c, mine), got)
    low_rank = half_done + low_rank(1 - c, got)
    moved = [wide(v) * (4.0 / BASE) for v in moved]
    even, odd = moved[0] + moved[2], moved[1] + moved[3]
    flip = l % 2 == 1
    base = jnp.concatenate([jnp.where(flip, odd, even), jnp.where(flip, even, odd)], axis=1)
    return (base + low_rank, grad.T)


def solution(mesh):
    fine = Mesh(mesh.devices.reshape(SIZES), AXES)
    dp, mp = ("x", "l"), ("y", "h", "c")
    in_specs = (P(dp, mp), P(dp, mp), P(dp, mp), P(None, mp), P(None, mp), P(), P(dp))
    out_specs = (P(dp, mp), P(None, mp))
    return jax.shard_map(
        on_device, mesh=fine, in_specs=in_specs, out_specs=out_specs, check_vma=False
    )
```
